32 devices in a mesh: seq: 8 (over z, y), fsdp: 4 (over x, core).
Axes of the slice: x: 2, y: 2, z: 4, core: 2. Of those that a mesh axis runs over, the one named last changes fastest.
Arguments:
- tokens: bfloat16 [4, 8192, 768], P('fsdp', 'seq'), may hold values from -6 to 6
- in_weight: bfloat16 [768, 3352], P('fsdp'), may hold values from -0.21875 to 0.21875
- out_weight: bfloat16 [1536, 768], P('fsdp'), may hold values from -0.15625 to 0.15625
- conv_weight: bfloat16 [1792, 4], P('fsdp'), may hold values from -3 to 3
- conv_bias: bfloat16 [1792], P('fsdp'), may hold values from -3 to 3
- step_bias: bfloat16 [24], P('fsdp'), may hold values from -4 to -1
- decay_param: bfloat16 [24], P('fsdp'), may hold values from -7 to -0.5
- skip_gain: bfloat16 [24], P('fsdp'), may hold values from 0.5 to 1.5
- norm_gain: bfloat16 [768], P('fsdp'), may hold values from 0.099609375 to 1.8984375
- gate_gain: bfloat16 [1536], P('fsdp'), may hold values from 0.099609375 to 1.8984375
- cotangent: bfloat16 [4, 8192, 768], P('fsdp', 'seq'), may hold values from -6 to 6
Outputs:
- block_out: bfloat16 [4, 8192, 768], P('fsdp', 'seq')
- grad_input: bfloat16 [4, 8192, 768], P('fsdp', 'seq')
- grad_inproj: float32 [768, 3352], P('fsdp')
- grad_outproj: float32 [1536, 768], P('fsdp')
- grad_conv: float32 [1792, 4], P('fsdp')
- grad_convbias: float32 [1792], P('fsdp')
- grad_stepbias: float32 [24], P('fsdp')
- grad_decay: float32 [24], P('fsdp')
- grad_skip: float32 [24], P('fsdp')
- grad_normgain: float32 [768], P('fsdp')
- grad_gategain: float32 [1536], P('fsdp')
The draws below stay inside these ranges and needn't reach their ends.
All inputs are finite; a program needn't handle non-finite values.
Results may differ from the reference program's by a relative error of at most 0.0033.
The reference program's roundings to bfloat16 on the way count: a program that leaves them out, or rounds other values in their place, can miss the bound.
Values may be sent and summed in bfloat16 or wider, within the bound.
A program may use at most 256 MiB of HBM per device.

```python
import jax
import jax.numpy as jnp
from jax import lax

D = 768
HEADS = 24
HEADDIM = 64
NSTATE = 128
CONV = 4
SPAN = 256
DI = 1536
CONVDIM = 1792
PROJ = 3352
SEQS = 4
LENGTH = 8192


def shard_levels(key, dims, cuts, least, top_value):
    def one(axis_at, parts):
        draws = jax.random.uniform(jax.random.fold_in(jax.random.fold_in(key, 6), axis_at), (parts,), jnp.float32, least / len(cuts), top_value / len(cuts))
        return jnp.repeat(jnp.exp(draws), dims[axis_at] // parts).reshape((-1,) + (1,) * (len(dims) - axis_at - 1))

    gain = one(*cuts[0])
    for cut in cuts[1:]:
        gain = gain * one(*cut)
    return gain


def scatter_about(stream_key, shape, scale, limit, split=(), kind=jnp.bfloat16):
    gain = shard_levels(stream_key, shape, split, -0.22, 0.18) if split else 1.0
    values = jax.random.normal(stream_key, shape, jnp.float32) * scale * gain
    return jnp.minimum(jnp.maximum(values, -limit), limit).astype(kind)


def setup_inputs(seed: int = 0) -> dict:
    arg_keys = jax.random.split(jax.random.key(seed), 12)
    return {
        "tokens": scatter_about(arg_keys[0], (SEQS, LENGTH, D), 1.0, 6.0, ((0, 4), (1, 8))),
        "in_weight": scatter_about(arg_keys[1], (D, PROJ), D ** -0.5, 0.21875, ((0, 4),)),
        "out_weight": scatter_about(arg_keys[2], (DI, D), DI ** -0.5, 0.15625, ((0, 4),)),
        "conv_weight": scatter_about(arg_keys[3], (CONVDIM, CONV), CONV ** -0.5, 3.0, ((0, 4),)),
        "conv_bias": scatter_about(arg_keys[4], (CONVDIM,), 0.3, 3.0, ((0, 4),)),
        "step_bias": jnp.clip(-4.0 + 3.0 * jax.random.uniform(arg_keys[5], (HEADS,), jnp.float32) ** shard_levels(arg_keys[5], (HEADS,), ((0, 4),), -0.2, 0.2), -4.0, -1.0).astype(jnp.bfloat16),
        "decay_param": jnp.clip(-7.0 + 6.5 * jax.random.uniform(arg_keys[6], (HEADS,), jnp.float32) ** shard_levels(arg_keys[6], (HEADS,), ((0, 4),), -0.2, 0.2), -7.0, -0.5).astype(jnp.bfloat16),
        "skip_gain": jnp.clip(0.5 + 1.0 * jax.random.uniform(arg_keys[7], (HEADS,), jnp.float32) ** shard_levels(arg_keys[7], (HEADS,), ((0, 4),), -0.2, 0.2), 0.5, 1.5).astype(jnp.bfloat16),
        "norm_gain": jnp.clip(1.0 + 0.18 * jax.random.normal(arg_keys[8], (D,), jnp.float32), 0.099609375, 1.8984375).astype(jnp.bfloat16),
        "gate_gain": jnp.clip(1.0 + 0.18 * jax.random.normal(arg_keys[9], (DI,), jnp.float32), 0.099609375, 1.8984375).astype(jnp.bfloat16),
        "cotangent": scatter_about(arg_keys[10], (SEQS, LENGTH, D), 1.0, 6.0, ((0, 4), (1, 8))),
    }


epsilon = 1e-05
highest = lax.Precision.HIGHEST

@jax.custom_vjp
def low(v):
    return lax.optimization_barrier(v.astype(jnp.bfloat16)).astype(jnp.float32)

@jax.custom_vjp
def low_back(v):
    return v

def low_keep(v):
    return (low(v), None)

def low_pass(kept, grad):
    return (grad,)

def back_keep(v):
    return (v, None)

def back_low(kept, grad):
    return (low(grad),)
low.defvjp(low_keep, low_pass)
low_back.defvjp(back_keep, back_low)

def advance(state, pieces):
    values, write_rows, read_rows, dt_step, decay_log = pieces
    cumulative = jnp.cumsum(decay_log, axis=0)
    positions = jnp.arange(SPAN)
    causal = (positions[:, None] >= positions[None, :])[:, :, None]
    spread = jnp.where(causal, cumulative[:, None, :] - cumulative[None, :, :], 0.0)
    kernel = jnp.where(causal, jnp.exp(spread), 0.0)
    scores = jnp.dot(read_rows, write_rows.T, precision=highest)
    weights = scores[:, :, None] * kernel * dt_step[None, :, :]
    inner_part = jnp.einsum('tsh,shp->thp', weights, values, precision=highest)
    carried = jnp.exp(cumulative)[:, :, None] * jnp.einsum('tn,hpn->thp', read_rows, state, precision=highest)
    tail_weight = jnp.exp(cumulative[-1][None, :] - cumulative) * dt_step
    new_state = jnp.exp(cumulative[-1])[:, None, None] * state + jnp.einsum('sh,shp,sn->hpn', tail_weight, values, write_rows, precision=highest)
    return (new_state, inner_part + carried)

def state_mix(values, write_rows, read_rows, dt_step, decay_log):
    length = values.shape[0]
    count = length // SPAN
    pieces = (values.reshape(count, SPAN, HEADS, HEADDIM), write_rows.reshape(count, SPAN, NSTATE), read_rows.reshape(count, SPAN, NSTATE), dt_step.reshape(count, SPAN, HEADS), decay_log.reshape(count, SPAN, HEADS))
    start = jnp.zeros((HEADS, HEADDIM, NSTATE), jnp.float32)
    _, mixed = lax.scan(jax.checkpoint(advance), start, pieces)
    return mixed.reshape(length, HEADS, HEADDIM)

def block_forward(source, in_weight, out_weight, conv_weight, conv_bias, step_bias, decay_param, skip_gain, norm_gain, gate_gain):
    length = source.shape[0]
    in_scale = lax.rsqrt(lax.optimization_barrier(jnp.mean(source * source, axis=1, keepdims=True)) + epsilon)
    normed = low(source * in_scale * norm_gain)
    projected = low_back(low(jnp.dot(normed, in_weight, precision=highest)))
    gate_part = projected[:, :DI]
    conv_in = projected[:, DI:DI + CONVDIM]
    step_raw = projected[:, DI + CONVDIM:]
    padded = jnp.concatenate([jnp.zeros((CONV - 1, CONVDIM), jnp.float32), conv_in], axis=0)
    conv_sum = conv_bias[None, :] + jnp.zeros((length, CONVDIM), jnp.float32)
    for tap_index in range(CONV):
        conv_sum = conv_sum + conv_weight[:, tap_index] * padded[tap_index:tap_index + length]
    conv_out = jax.nn.silu(conv_sum)
    values = conv_out[:, :DI].reshape(length, HEADS, HEADDIM)
    write_rows = conv_out[:, DI:DI + NSTATE]
    read_rows = conv_out[:, DI + NSTATE:]
    dt_step = jax.nn.softplus(step_raw + step_bias)
    decay_log = -dt_step * jnp.exp(decay_param)
    mixed = state_mix(values, write_rows, read_rows, dt_step, decay_log) + skip_gain[None, :, None] * values
    gated = mixed.reshape(length, DI) * jax.nn.silu(gate_part)
    gate_scale = lax.rsqrt(lax.optimization_barrier(jnp.mean(gated * gated, axis=1, keepdims=True)) + epsilon)
    normed_out = low(gated * gate_scale * gate_gain)
    return source + jnp.dot(normed_out, out_weight, precision=highest)

def reference(tokens, in_weight, out_weight, conv_weight, conv_bias, step_bias, decay_param, skip_gain, norm_gain, gate_gain, cotangent):
    params = (in_weight.astype(jnp.float32), out_weight.astype(jnp.float32), conv_weight.astype(jnp.float32), conv_bias.astype(jnp.float32), step_bias.astype(jnp.float32), decay_param.astype(jnp.float32), skip_gain.astype(jnp.float32), norm_gain.astype(jnp.float32), gate_gain.astype(jnp.float32))

    def one_sequence(totals, pair):
        seq_in, seq_cot = pair
        result, pullback = jax.vjp(block_forward, seq_in.astype(jnp.float32), *params)
        grads = pullback(seq_cot.astype(jnp.float32))
        summed = tuple((total + grad for total, grad in zip(totals, grads[1:])))
        return (summed, (result.astype(jnp.bfloat16), grads[0].astype(jnp.bfloat16)))
    start = tuple((jnp.zeros_like(param) for param in params))
    totals, (block_out, grad_input) = lax.scan(one_sequence, start, (tokens, cotangent))
    return (block_out, grad_input, totals[0], totals[1], totals[2], totals[3], totals[4], totals[5], totals[6], totals[7], totals[8])
```

```python
import functools

import jax
import jax.numpy as jnp
from jax import lax
from jax.experimental import pallas as pl
from jax.experimental.pallas import tpu as pltpu
from jax.sharding import PartitionSpec as P

SPAN = 256
LANES = 128

epsilon = 1e-05
highest = lax.Precision.HIGHEST
f32 = jnp.float32
bf16 = jnp.bfloat16

NN = (((1,), (0,)), ((), ()))
NT = (((1,), (1,)), ((), ()))
TN = (((0,), (0,)), ((), ()))


def split(a):
    high = a.astype(bf16)
    return high, (a - high.astype(f32)).astype(bf16)


def mm3(a, b, dims):
    ah, al = a
    bh, bl = b
    dot = functools.partial(lax.dot_general, dimension_numbers=dims, preferred_element_type=f32)
    return dot(ah, bh) + (dot(ah, bl) + dot(al, bh))


def masked(pair, keep):
    return tuple(jnp.where(keep, part, jnp.zeros_like(part)) for part in pair)


def pick(lane_first, cols, a, b):
    return jnp.where(lane_first, cols[:, a : a + 1], cols[:, b : b + 1])


def forward_kernel(v_ref, w_ref, r_ref, rows_ref, first_ref, skip_ref, y_ref, ent_ref, state, scores):
    pair, chunk = pl.program_id(0), pl.program_id(1)
    w = split(w_ref[...])
    r = split(r_ref[...])

    @pl.when(pair == 0)
    def _():
        scores[chunk] = mm3(r, w, NT)

    @pl.when(chunk == 0)
    def _():
        state[...] = first_ref[...]

    rows = rows_ref[0, 0]
    cols = rows.T
    span = rows.shape[1]
    lane_first = lax.broadcasted_iota(jnp.int32, (1, LANES), 1) < LANES // 2
    causal = lax.broadcasted_iota(jnp.int32, (span, span), 0) >= lax.broadcasted_iota(
        jnp.int32, (span, span), 1
    )
    values = v_ref[...]
    v = split(values)
    held = state[...]
    ent_ref[0] = held
    scored = scores[chunk]
    total = pick(lane_first, cols, 0, 1)
    y = jnp.exp(total) * mm3(r, split(held), NN) + skip_ref[...] * values
    for head in range(2):
        gap = jnp.where(causal, cols[:, head : head + 1] - rows[head : head + 1], 0.0)
        weights = jnp.where(causal, jnp.exp(gap) * scored * rows[2 + head : 3 + head], 0.0)
        keep = lane_first if head == 0 else jnp.logical_not(lane_first)
        y = y + mm3(split(weights), masked(v, keep), NN)
    y_ref[...] = y
    last = total[span - 1 : span]
    tail = jnp.exp(last - total) * pick(lane_first, cols, 2, 3)
    state[...] = jnp.exp(last) * held + mm3(w, split(tail * values), TN)


def backward_kernel(
    v_ref, w_ref, r_ref, rows_ref, first_ref, skip_ref, ent_ref, gm_ref,
    gv_ref, gw_ref, gr_ref, out_ref,
    state, scores, score_grads,
):
    pair, lap = pl.program_id(0), pl.program_id(1)
    chunk = pl.num_programs(1) - 1 - lap
    w = split(w_ref[...])
    r = split(r_ref[...])
    rows = rows_ref[0, 0]
    cols = rows.T
    span = rows.shape[1]
    here = pl.ds(pl.multiple_of(chunk * span, span), span)

    @pl.when(pair == 0)
    def _():
        scores[chunk] = mm3(r, w, NT)
        score_grads[chunk] = jnp.zeros((span, span), f32)
        gw_ref[here, :] = jnp.zeros((span, LANES), f32)
        gr_ref[here, :] = jnp.zeros((span, LANES), f32)

    @pl.when(lap == 0)
    def _():
        state[...] = first_ref[...]

    lane = lax.broadcasted_iota(jnp.int32, (1, LANES), 1)
    lane_first = lane < LANES // 2
    causal = lax.broadcasted_iota(jnp.int32, (span, span), 0) >= lax.broadcasted_iota(
        jnp.int32, (span, span), 1
    )
    values = v_ref[...]
    v = split(values)
    grad_mixed = gm_ref[...]
    g = split(grad_mixed)
    entering = ent_ref[0]
    ent = split(entering)
    leaving = state[...]
    leav = split(leaving)
    scored = scores[chunk]
    total = pick(lane_first, cols, 0, 1)
    last = total[span - 1 : span]
    grown = jnp.exp(total) * grad_mixed
    gg = split(grown)
    fading = jnp.exp(last - total)
    tail = fading * pick(lane_first, cols, 2, 3)
    tv = split(tail * values)
    carried = grown * mm3(r, ent, NN)
    state_rows = mm3(w, leav, NN)
    ending = state_rows * values * fading
    grad_values = skip_ref[...] * grad_mixed + tail * state_rows
    joined = jnp.sum(leaving * (jnp.exp(last) * entering), axis=0, keepdims=True)
    back = jnp.zeros((span, LANES), f32)
    sums = []
    grads = score_grads[chunk]
    for head in range(2):
        keep = lane_first if head == 0 else jnp.logical_not(lane_first)
        gap = jnp.where(causal, cols[:, head : head + 1] - rows[head : head + 1], 0.0)
        kernel = jnp.where(causal, jnp.exp(gap), 0.0)
        step = rows[2 + head : 3 + head]
        gh = masked(g, keep)
        weights = split(scored * kernel * step)
        grad_values = grad_values + mm3(weights, gh, TN)
        shaped = mm3(gh, v, NT) * kernel
        grads = grads + shaped * step
        products = shaped * scored
        sums.append(jnp.sum(products, axis=0, keepdims=True))
        by_row = jnp.sum(products * step, axis=1, keepdims=True) + jnp.sum(
            jnp.where(keep, carried, 0.0), axis=1, keepdims=True
        )
        by_end = jnp.sum(jnp.where(keep, ending, 0.0), axis=1, keepdims=True)
        whole = jnp.sum(jnp.where(keep, joined, 0.0), axis=1, keepdims=True)
        back = jnp.where(lane == head, by_row, back)
        back = jnp.where(lane == 2 + head, by_end, back)
        back = jnp.where(lane == 6 + head, whole, back)
    score_grads[chunk] = grads
    gv_ref[...] = grad_values
    out_ref[0, 0] = back.T[:8]
    out_ref[0, 0, 4:5, :] = sums[0]
    out_ref[0, 0, 5:6, :] = sums[1]
    gr_ref[here, :] += mm3(gg, ent, NT)
    gw_ref[here, :] += mm3(tv, leav, NT)
    state[...] = mm3(r, gg, TN) + jnp.exp(last) * leaving

    @pl.when(pair == pl.num_programs(0) - 1)
    def _():
        s = split(grads)
        gr_ref[here, :] += mm3(s, w, NN)
        gw_ref[here, :] += mm3(s, r, TN)


def scan_forward(values, write_rows, read_rows, rows, first, skip_row):
    length, width = values.shape
    pairs, spans = rows.shape[0], rows.shape[1]
    states = first.shape[0]
    wide = pl.BlockSpec((SPAN, LANES), lambda p, c: (c, p))
    thin = pl.BlockSpec((SPAN, states), lambda p, c: (c, 0))
    return pl.pallas_call(
        forward_kernel,
        grid=(pairs, spans),
        in_specs=[
            wide, thin, thin,
            pl.BlockSpec((1, 1, 8, SPAN), lambda p, c: (p, c, 0, 0)),
            pl.BlockSpec((states, LANES), lambda p, c: (0, p)),
            pl.BlockSpec((1, LANES), lambda p, c: (0, p)),
        ],
        out_specs=[wide, pl.BlockSpec((1, states, LANES), lambda p, c: (c, 0, p))],
        out_shape=[
            jax.ShapeDtypeStruct((length, width), f32),
            jax.ShapeDtypeStruct((spans, states, width), f32),
        ],
        scratch_shapes=[pltpu.VMEM((states, LANES), f32), pltpu.VMEM((spans, SPAN, SPAN), f32)],
        compiler_params=pltpu.CompilerParams(vmem_limit_bytes=32 * 1024 * 1024),
        name="scan_forward",
    )(values, write_rows, read_rows, rows, first, skip_row)


def scan_backward(values, write_rows, read_rows, rows, first, skip_row, entering, grad_mixed):
    length, width = values.shape
    pairs, spans = rows.shape[0], rows.shape[1]
    states = first.shape[0]
    end = spans - 1
    wide = pl.BlockSpec((SPAN, LANES), lambda p, c: (end - c, p))
    thin = pl.BlockSpec((SPAN, states), lambda p, c: (end - c, 0))
    whole = pl.BlockSpec((length, states), lambda p, c: (0, 0))
    lines = pl.BlockSpec((1, 1, 8, SPAN), lambda p, c: (p, end - c, 0, 0))
    return pl.pallas_call(
        backward_kernel,
        grid=(pairs, spans),
        in_specs=[
            wide, thin, thin, lines,
            pl.BlockSpec((states, LANES), lambda p, c: (0, p)),
            pl.BlockSpec((1, LANES), lambda p, c: (0, p)),
            pl.BlockSpec((1, states, LANES), lambda p, c: (end - c, 0, p)),
            wide,
        ],
        out_specs=[wide, whole, whole, lines],
        out_shape=[
            jax.ShapeDtypeStruct((length, width), f32),
            jax.ShapeDtypeStruct((length, states), f32),
            jax.ShapeDtypeStruct((length, states), f32),
            jax.ShapeDtypeStruct((pairs, spans, 8, SPAN), f32),
        ],
        scratch_shapes=[
            pltpu.VMEM((states, LANES), f32),
            pltpu.VMEM((spans, SPAN, SPAN), f32),
            pltpu.VMEM((spans, SPAN, SPAN), f32),
        ],
        compiler_params=pltpu.CompilerParams(vmem_limit_bytes=32 * 1024 * 1024),
        name="scan_backward",
    )(values, write_rows, read_rows, rows, first, skip_row, entering, grad_mixed)


def from_behind(array, axis, by):
    devices = lax.axis_size(axis)
    pairs = [(i, i + by) for i in range(devices) if 0 <= i + by < devices]
    return lax.ppermute(array, axis, pairs)


def swap(array, axis):
    return lax.all_to_all(array, axis, 0, 0, tiled=True)


def prefix(part, logs, widen, reverse):
    count = logs.shape[0]
    states, width = part.shape
    parts = swap(part, "seq").reshape(count, states // count, width)
    ends = jnp.cumsum(logs, axis=0)
    place = jnp.arange(count)
    if reverse:
        used = place[None, :] > place[:, None]
        gaps = (ends - logs)[None, :] - ends[:, None]
    else:
        used = place[None, :] < place[:, None]
        gaps = (ends - logs)[:, None] - ends[None, :]
    used = used[:, :, None]
    factors = jnp.where(used, jnp.exp(jnp.where(used, gaps, 0.0)), 0.0)
    factors = widen(factors.reshape(count * count, -1)).reshape(count, count, 1, width)
    total = jnp.sum(factors * parts[None], axis=1)
    return swap(total.reshape(states, width), "seq")


def gather_sum(grad):
    owners = lax.axis_size("fsdp")
    pieces = lax.axis_size("seq")
    rows, width = grad.shape
    share = swap(grad.astype(bf16), "fsdp").reshape(owners, rows // owners, width)
    share = jnp.sum(share.astype(f32), axis=0)
    parts = swap(share.astype(bf16), "seq").reshape(pieces, rows // owners // pieces, width)
    part = jnp.sum(parts.astype(f32), axis=0)
    return lax.all_gather(part, "seq", axis=0, tiled=True)


def plain_sum(grad):
    share = lax.psum_scatter(grad, "fsdp", scatter_dimension=0, tiled=True)
    return lax.psum(share, "seq")


def silu_slope(inputs):
    sig_value = jax.nn.sigmoid(inputs)
    return sig_value * (1.0 + inputs * (1.0 - sig_value))


def on_device(
    tokens, in_weight, out_weight, conv_weight, conv_bias, step_bias,
    decay_param, skip_gain, norm_gain, gate_gain, cotangent,
):
    smalls = (conv_weight.reshape(-1), conv_bias, step_bias, decay_param, skip_gain, norm_gain, gate_gain)
    sizes = [a.shape[0] for a in smalls]
    offsets = [sum(sizes[:i]) for i in range(len(sizes) + 1)]
    packed = lax.all_gather(jnp.concatenate(smalls)[None], "fsdp", axis=0, tiled=True).astype(f32)
    full = [packed[:, offsets[i] : offsets[i + 1]].reshape(-1) for i in range(len(sizes))]
    tap_count = conv_weight.shape[1]
    conv_taps = full[0].reshape(-1, tap_count)
    conv_offset, step_offset, decay_values, skip_values, gain_in, gain_out = full[1:]
    full_in = lax.all_gather(in_weight, "fsdp", axis=0, tiled=True)
    full_out = lax.all_gather(out_weight, "fsdp", axis=0, tiled=True)
    length = tokens.shape[1]
    head_count = step_offset.shape[0]
    inner_width = full_out.shape[0]
    conv_width = conv_taps.shape[0]
    state_dim = (conv_width - inner_width) // 2
    head_dim = inner_width // head_count
    span_count = length // SPAN
    pairs = head_count // 2
    spread = (jnp.arange(inner_width)[None, :] // head_dim == jnp.arange(head_count)[:, None]).astype(f32)

    def widen(a):
        return jnp.dot(a, spread, precision=highest)

    source = tokens[0].astype(f32)
    in_scale = lax.rsqrt(jnp.mean(source * source, axis=1, keepdims=True) + epsilon)
    normed = (source * in_scale * gain_in).astype(bf16)
    projected = jnp.dot(normed, full_in, preferred_element_type=f32).astype(bf16)
    gate_part = projected[:, :inner_width].astype(f32)
    conv_in = projected[:, inner_width : inner_width + conv_width]
    step_raw = projected[:, inner_width + conv_width :].astype(f32)
    rim = tap_count - 1
    rim_rows = from_behind(conv_in[length - rim :], "seq", 1)
    lead = 16
    extended = jnp.concatenate(
        [jnp.zeros((lead - rim, conv_width), bf16), rim_rows, conv_in], axis=0
    ).astype(f32)
    shifted = [extended[lead - rim + k : lead - rim + k + length] for k in range(tap_count)]
    conv_sum = conv_offset[None, :] + sum(conv_taps[:, k] * shifted[k] for k in range(tap_count))
    conv_out = jax.nn.silu(conv_sum)
    values = conv_out[:, :inner_width]
    write_rows = conv_out[:, inner_width : inner_width + state_dim]
    read_rows = conv_out[:, inner_width + state_dim :]
    step_pre = step_raw + step_offset
    dt_step = jax.nn.softplus(step_pre)
    decay_rate = -jnp.exp(decay_values)
    decay_log = dt_step * decay_rate
    cumulative = jnp.cumsum(decay_log.reshape(span_count, SPAN, head_count), axis=1)
    span_log = cumulative[:, -1]
    prior_log = jnp.cumsum(span_log, axis=0) - span_log
    device_log = jnp.sum(span_log, axis=0)
    along = (cumulative + prior_log[:, None, :]).reshape(length, head_count)
    logs = lax.all_gather(device_log, "seq")

    def as_rows(a):
        return a.reshape(span_count, SPAN, pairs, 2).transpose(2, 0, 3, 1)

    step_rows = as_rows(dt_step)
    rows = jnp.concatenate(
        [as_rows(cumulative), step_rows, jnp.zeros((pairs, span_count, 4, SPAN), f32)], axis=2
    )
    skip_row = widen(skip_values[None])
    tail = widen(jnp.exp(device_log[None, :] - along) * dt_step)
    final_local = lax.dot_general(write_rows, tail * values, TN, precision=highest)
    incoming = prefix(final_local, logs, widen, False)
    flat, entering = scan_forward(values, write_rows, read_rows, rows, incoming, skip_row)
    gate_silu = jax.nn.silu(gate_part)
    gated = flat * gate_silu
    gate_scale = lax.rsqrt(jnp.mean(gated * gated, axis=1, keepdims=True) + epsilon)
    normed_out = (gated * gate_scale * gain_out).astype(bf16)
    block_out = source + jnp.dot(normed_out, full_out, preferred_element_type=f32)
    grad_out = cotangent[0]
    grad_outproj = jnp.einsum("ti,td->id", normed_out, grad_out, preferred_element_type=f32)
    grad_normed = jnp.einsum("td,id->ti", grad_out, full_out, preferred_element_type=f32)
    grad_gategain = jnp.sum(grad_normed * gated * gate_scale, axis=0)
    grad_scaled = grad_normed * gain_out
    grad_gated = gate_scale * grad_scaled - gated * gate_scale**3 * jnp.mean(
        grad_scaled * gated, axis=1, keepdims=True
    )
    grad_gate = (grad_gated * flat * silu_slope(gate_part)).astype(bf16)
    grad_mixed = grad_gated * gate_silu
    grad_skip = jnp.sum(jnp.sum(grad_mixed * values, axis=0).reshape(head_count, head_dim), axis=1)
    start_grad = lax.dot_general(read_rows, widen(jnp.exp(along)) * grad_mixed, TN, precision=highest)
    outgoing = prefix(start_grad, logs, widen, True)
    grad_outproj = plain_sum(grad_outproj)
    grad_gateproj = plain_sum(
        jnp.einsum("td,tk->dk", normed, grad_gate, preferred_element_type=f32)
    )
    grad_values, grad_write, grad_read, back = scan_backward(
        values, write_rows, read_rows, rows, outgoing, skip_row, entering, grad_mixed
    )
    flowing = jnp.sum(back[:, :, 2:4] * step_rows, axis=3)
    grad_cumul = back[:, :, 0:2] - step_rows * (back[:, :, 2:4] + back[:, :, 4:6])
    behind = jnp.sum(grad_cumul, axis=3, keepdims=True) - jnp.cumsum(grad_cumul, axis=3) + grad_cumul
    grad_log = behind + (flowing + back[:, :, 6:8, 0])[..., None]

    def from_rows(a):
        return a.transpose(1, 3, 0, 2).reshape(length, head_count)

    grad_decaylog = from_rows(grad_log)
    grad_step = from_rows(back[:, :, 2:4] + back[:, :, 4:6]) + grad_decaylog * decay_rate
    grad_decay = jnp.sum(grad_decaylog * dt_step, axis=0) * decay_rate
    grad_pre = grad_step * jax.nn.sigmoid(step_pre)
    grad_stepbias = jnp.sum(grad_pre, axis=0)
    grad_sum = jnp.concatenate([grad_values, grad_write, grad_read], axis=1) * silu_slope(conv_sum)
    grad_convbias = jnp.sum(grad_sum, axis=0)
    grad_conv = jnp.stack([jnp.sum(grad_sum * shifted[k], axis=0) for k in range(tap_count)], axis=1)
    next_rows = from_behind(grad_sum[:rim], "seq", -1)
    reaching = jnp.concatenate([grad_sum, next_rows], axis=0)
    grad_conv_in = sum(conv_taps[:, k] * reaching[rim - k : rim - k + length] for k in range(tap_count))
    grad_rest = jnp.concatenate([grad_conv_in, grad_pre], axis=1).astype(bf16)
    grad_restproj = jnp.einsum("td,tk->dk", normed, grad_rest, preferred_element_type=f32)
    grad_normed_in = jnp.einsum(
        "tk,dk->td", grad_gate, full_in[:, :inner_width], preferred_element_type=f32
    ) + jnp.einsum("tk,dk->td", grad_rest, full_in[:, inner_width:], preferred_element_type=f32)
    grad_normgain = jnp.sum(grad_normed_in * source * in_scale, axis=0)
    grad_scaled_in = grad_normed_in * gain_in
    grad_source = in_scale * grad_scaled_in - source * in_scale**3 * jnp.mean(
        grad_scaled_in * source, axis=1, keepdims=True
    )
    grad_source = grad_source + grad_out.astype(f32)
    owners = lax.axis_size("fsdp")
    small_grads = (
        grad_conv.reshape(-1), grad_convbias, grad_stepbias, grad_decay,
        grad_skip, grad_normgain, grad_gategain,
    )
    small = jnp.concatenate([a.reshape(owners, -1) for a in small_grads], axis=1)
    small = lax.psum(small, ("fsdp", "seq"))
    mine = lax.dynamic_index_in_dim(small, lax.axis_index("fsdp"), 0, False)
    shares = [mine[offsets[i] : offsets[i + 1]] for i in range(len(sizes))]
    grad_inproj = jnp.concatenate([grad_gateproj, gather_sum(grad_restproj)], axis=1)
    return (
        block_out[None].astype(bf16),
        grad_source[None].astype(bf16),
        grad_inproj,
        grad_outproj,
        shares[0].reshape(-1, tap_count),
        *shares[1:],
    )


def solution(mesh):
    placed = (
        P("fsdp", "seq", None),
        P("fsdp", None),
        P("fsdp", None),
        P("fsdp", None),
        P("fsdp"),
        P("fsdp"),
        P("fsdp"),
        P("fsdp"),
        P("fsdp"),
        P("fsdp"),
        P("fsdp", "seq", None),
    )
    return jax.shard_map(
        on_device,
        mesh=mesh,
        in_specs=placed,
        out_specs=(
            P("fsdp", "seq", None),
            P("fsdp", "seq", None),
            P("fsdp", None),
            P("fsdp", None),
            P("fsdp", None),
            P("fsdp"),
            P("fsdp"),
            P("fsdp"),
            P("fsdp"),
            P("fsdp"),
            P("fsdp"),
        ),
        check_vma=False,
    )
```
